512 devices in a mesh: row: 32 (over z, x), src: 16 (over y, core).
Axes of the slice: x: 4, y: 8, z: 8, core: 2. Of those that a mesh axis runs over, the one named last changes fastest.
Arguments:
- shot_fields: bfloat16 [2, 2, 4096, 2048], P(None, None, ('row', 'src')), may hold values from -6 to 6
- diag_inverse: bfloat16 [2, 2, 2048, 2048], P(None, None, 'row', 'src'), may hold values from -0.09375 to 0.09375
- coupling: bfloat16 [2, 2048, 2048], P(None, 'row', 'src'), may hold values from -0.09375 to 0.09375
Outputs:
- solved: bfloat16 [2, 2, 4096, 2048], P(None, None, ('row', 'src'))
The draws below stay inside these ranges and needn't reach their ends.
All inputs are finite; a program needn't handle non-finite values.
Results may differ from the reference program's by a relative error of at most 0.0049.
Values may be sent and summed in bfloat16 or wider, within the bound.
No kernel may reach another device: no remote copies, remote signals or barrier semaphores. Data moves between devices by JAX's collectives and lax.ppermute only.
A program may use at most 64 MiB of HBM per device.

```python
import jax
import jax.numpy as jnp

PANEL = 2048
PANELS = 2
SOURCES = 4096


def steps_of(own_key, dims, shards, least, top_value):
    def one(position, parts):
        draws = jax.random.uniform(jax.random.fold_in(jax.random.fold_in(own_key, 6), position), (parts,), jnp.float32, least / len(shards), top_value / len(shards))
        return jnp.repeat(jnp.exp(draws), dims[position] // parts).reshape((-1,) + (1,) * (len(dims) - position - 1))

    loudness = one(*shards[0])
    for cut in shards[1:]:
        loudness = loudness * one(*cut)
    return loudness


def scatter_about(rng, dims, deviation, most, shards=(), kind=jnp.bfloat16):
    gain = steps_of(rng, dims, shards, -0.22, 0.18) if shards else 1.0
    entries = jax.random.normal(rng, dims, jnp.float32) * deviation * gain
    return jnp.minimum(jnp.maximum(entries, -most), most).astype(kind)


def setup_inputs(seed: int = 0) -> dict:
    streams_of = jax.random.split(jax.random.key(seed), 4)
    return {
        "shot_fields": scatter_about(streams_of[0], (2, PANELS, SOURCES, PANEL), 1.0, 6.0, ((2, 512),)),
        "diag_inverse": scatter_about(streams_of[1], (2, PANELS, PANEL, PANEL), (2 * PANEL) ** -0.5, 0.09375, ((2, 32), (3, 16))),
        "coupling": scatter_about(streams_of[2], (2, PANEL, PANEL), (2 * PANEL) ** -0.5, 0.09375, ((1, 32), (2, 16))),
    }


def complex_product(matrix, vector):
    products = jnp.einsum('csk,drk->cdsr', vector.astype(jnp.float32), matrix.astype(jnp.float32))
    return jnp.stack([products[0, 0] - products[1, 1], products[1, 0] + products[0, 1]], axis=0)


def reference(shot_fields, diag_inverse, coupling):
    first_sol = complex_product(diag_inverse[:, 0], shot_fields[:, 0]).astype(jnp.bfloat16)
    update = complex_product(coupling, first_sol)
    residual = (shot_fields[:, 1].astype(jnp.float32) - update).astype(jnp.bfloat16)
    second_sol = complex_product(diag_inverse[:, 1], residual).astype(jnp.bfloat16)
    return jnp.stack([first_sol, second_sol], axis=1)
```

```python
import functools

import jax
import jax.numpy as jnp
from jax import lax
from jax.experimental import pallas as pl
from jax.experimental.pallas import tpu as pltpu
from jax.sharding import Mesh, PartitionSpec as P

F32, BF16 = jnp.float32, jnp.bfloat16
ZH, ZL, X, Y, CORES = 4, 2, 4, 8, 2
GROUP = ZL * X
VMEM_BYTES = 40 * 1024 * 1024
VMEM = pl.BlockSpec(memory_space=pltpu.VMEM)
SMEM = pl.BlockSpec(memory_space=pltpu.SMEM)


def call(body, out_shape, n_in, scalars=0, scratch=(), in_specs=None, flops=0, moved=1 << 20):
    return pl.pallas_call(
        body,
        out_shape=out_shape,
        in_specs=in_specs or [SMEM] * scalars + [VMEM] * (n_in - scalars),
        out_specs=jax.tree.map(lambda _: VMEM, out_shape),
        scratch_shapes=list(scratch),
        compiler_params=pltpu.CompilerParams(vmem_limit_bytes=VMEM_BYTES),
        cost_estimate=pl.CostEstimate(flops=flops, bytes_accessed=moved, transcendentals=0),
    )


def pack_fields(b_ref, out_ref):
    for d in range(GROUP):
        for c in range(2):
            out_ref[d, c, :, 0:2048] = b_ref[c, 0]
            base = d * 64
            for core in range(CORES):
                parts = [
                    b_ref[c, 1, :, zh * 512 + base + core * 32 : zh * 512 + base + core * 32 + 32]
                    for zh in range(ZH)
                ]
                lo = 2048 + core * 128
                out_ref[d, c, :, lo : lo + 128] = jnp.concatenate(parts, axis=-1)


def pack_matrices(diag_ref, coup_ref, out_ref):
    for c in range(2):
        for half in range(CORES):
            rows = slice(half * 32, half * 32 + 32)
            out_ref[half, 0, c] = diag_ref[c, 0, rows]
            out_ref[half, 1, c] = coup_ref[c, rows]
            out_ref[half, 2, c] = diag_ref[c, 1, rows]


def place_matrix(m_ref, mat_ref, which):
    for y in range(Y):
        for core in range(CORES):
            col = (y * 2 + core) * 128
            for c in range(2):
                for zh in range(ZH):
                    row = c * 128 + zh * 32
                    mat_ref[row : row + 32, col : col + 128] = m_ref[y, zh, core, which, c]


def complex_parts(prod):
    real = prod[:128, :128] - prod[128:, 128:]
    imag = prod[:128, 128:] + prod[128:, :128]
    return real, imag


def first_stage(core_ref, own_ref, other_ref, m_ref, rep_ref, first_ref, slice_ref, mat_ref, vec_ref):
    core = core_ref[0]
    place_matrix(m_ref, mat_ref, 0)
    rows_at = pl.multiple_of(2048 + core * 128, 128)
    for ref, who in ((own_ref, core), (other_ref, 1 - core)):
        at = pl.multiple_of(who * 64, 64)
        for c in range(2):
            vec_ref[pl.ds(c * 128 + at, 64), :] = ref[:, c, :, 0:2048].reshape(64, 2048)
            slice_ref[c, pl.ds(at, 64), :] = ref[:, c, :, pl.ds(rows_at, 128)].reshape(64, 128)
    prod = lax.dot_general(
        mat_ref[...], vec_ref[...], (((1,), (1,)), ((), ())), preferred_element_type=F32
    )
    for c, part in enumerate(complex_parts(prod)):
        part = part.astype(BF16)
        for d in range(GROUP):
            rep_ref[d, c] = part
        first_ref[c] = part


def place_fields(core, own_ref, other_ref, vec_ref):
    for ref, who in ((own_ref, core), (other_ref, 1 - core)):
        for d in range(GROUP):
            for zh in range(ZH):
                at = pl.multiple_of(zh * 512 + d * 64 + who * 32, 32)
                for c in range(2):
                    vec_ref[pl.ds(at, 32), c * 128 : c * 128 + 128] = ref[d, c, zh * 32 : zh * 32 + 32]


def second_stage(core_ref, own_ref, other_ref, m_ref, slice_ref, rep_ref, mat_ref, vec_ref):
    place_matrix(m_ref, mat_ref, 0)
    place_fields(core_ref[0], own_ref, other_ref, vec_ref)
    prod = jnp.dot(mat_ref[...], vec_ref[...], preferred_element_type=F32)
    for c, part in enumerate(complex_parts(prod)):
        residual = (slice_ref[c].astype(F32).T - part).astype(BF16)
        for d in range(GROUP):
            rep_ref[d, c] = residual


def third_stage(core_ref, own_ref, other_ref, m_ref, first_ref, out_ref, mat_ref, vec_ref):
    place_matrix(m_ref, mat_ref, 0)
    place_fields(core_ref[0], own_ref, other_ref, vec_ref)
    prod = jnp.dot(mat_ref[...], vec_ref[...], preferred_element_type=F32)
    for c, part in enumerate(complex_parts(prod)):
        for p, value in ((0, first_ref[c].astype(F32)), (1, part)):
            out_ref[:, c, p] = value.T.reshape(CORES * GROUP, 8, 128).astype(BF16)


def unpack(in_ref, out_ref):
    for c in range(2):
        for p in range(2):
            for zh in range(ZH):
                for pair in range(GROUP // 2):
                    parts = [
                        in_ref[core, 2 * pair + d, c, p, :, zh * 32 : zh * 32 + 32]
                        for d in range(2)
                        for core in range(CORES)
                    ]
                    at = zh * 512 + pair * 128
                    out_ref[c, p, :, at : at + 128] = jnp.concatenate(parts, axis=-1)


def gather_group(block):
    own = lax.all_to_all(block, ("zl", "x"), 0, 0, tiled=True)
    return own, lax.ppermute(own, "core", [(0, 1), (1, 0)])


def on_device(shot_fields, diag_inverse, coupling):
    shape = jax.ShapeDtypeStruct
    core = lax.axis_index("core").reshape(1)

    mats = call(pack_matrices, shape((2, 3, 2, 32, 128), BF16), 2)(diag_inverse, coupling)
    mats = lax.all_to_all(mats, "core", 0, 0, tiled=True)
    mats = jnp.broadcast_to(mats[None], (ZH,) + mats.shape)
    mats = lax.all_to_all(mats, "zh", 0, 0, tiled=True)
    mats = lax.all_gather(mats, "y", axis=0)

    fields = call(pack_fields, shape((GROUP, 2, 8, 2304), BF16), 1)(shot_fields)
    own, other = gather_group(fields)

    scratch = [pltpu.VMEM((256, 2048), BF16), pltpu.VMEM((256, 2048), BF16)]
    flops = 2 * 256 * 256 * 2048

    def mat_spec(which):
        return pl.BlockSpec((Y, ZH, CORES, 1, 2, 32, 128), lambda i: (0, 0, 0, which, 0, 0, 0))

    def whole(a):
        return pl.BlockSpec(a, lambda i: (0,) * len(a))

    def stage(body, which, outs, *args):
        specs = [SMEM] + [whole(a.shape) for a in args[:2]] + [mat_spec(which)]
        specs += [whole(a.shape) for a in args[2:]]
        vec = (256, 2048) if which == 0 else (2048, 256)
        return pl.pallas_call(
            body,
            grid=(1,),
            out_shape=outs,
            in_specs=specs,
            out_specs=jax.tree.map(lambda o: whole(o.shape), outs),
            scratch_shapes=[pltpu.VMEM((256, 2048), BF16), pltpu.VMEM(vec, BF16)],
            compiler_params=pltpu.CompilerParams(vmem_limit_bytes=VMEM_BYTES),
            cost_estimate=pl.CostEstimate(flops=flops, bytes_accessed=3 << 20, transcendentals=0),
        )(core, args[0], args[1], mats, *args[2:])

    rep = shape((GROUP, 2, 128, 128), BF16)
    block = shape((2, 128, 128), BF16)
    first_rep, first, second_slice = stage(first_stage, 0, (rep, block, block), own, other)
    own, other = gather_group(first_rep)
    residual_rep = stage(second_stage, 1, rep, own, other, second_slice)
    own, other = gather_group(residual_rep)
    both = stage(third_stage, 2, shape((CORES * GROUP, 2, 2, 8, 128), BF16), own, other, first)

    both = lax.all_to_all(both.reshape(CORES, GROUP, 2, 2, 8, 128), "core", 0, 0, tiled=True)
    both = lax.all_to_all(both, ("zl", "x"), 1, 1, tiled=True)
    return call(unpack, shape((2, 2, 8, 2048), BF16), 1)(both)


def solution(mesh):
    axes = ("zh", "zl", "x", "y", "core")
    fine = Mesh(mesh.devices.reshape(ZH, ZL, X, Y, CORES), axes)
    row, src = ("zh", "zl", "x"), ("y", "core")
    in_specs = (
        P(None, None, row + src, None),
        P(None, None, row, src),
        P(None, row, src),
    )
    out_specs = P(None, None, row + src, None)
    return jax.shard_map(
        on_device, mesh=fine, in_specs=in_specs, out_specs=out_specs, check_vma=False
    )
```

```python
import jax
import jax.numpy as jnp
from jax import lax
from jax.experimental import pallas as pl
from jax.experimental.pallas import tpu as pltpu
from jax.sharding import Mesh, PartitionSpec as P

F32, BF16 = jnp.float32, jnp.bfloat16
ZH, ZL, X, Y, CORES = 4, 2, 4, 8, 2
GROUP = ZL * X
PANEL, SHOTS = 2048, 8
ROWS = PANEL // GROUP
COLS = PANEL // Y
GROUP_SHOTS = GROUP * SHOTS
VMEM_BYTES = 40 * 1024 * 1024
VMEM = pl.BlockSpec(memory_space=pltpu.VMEM)
SMEM = pl.BlockSpec(memory_space=pltpu.SMEM)
NT = (((1,), (1,)), ((), ()))


def call(body, outs, *args, scalars=0, scratch=(), flops=0, moved=1 << 20):
    return pl.pallas_call(
        body,
        out_shape=outs,
        in_specs=[SMEM] * scalars + [VMEM] * (len(args) - scalars),
        out_specs=jax.tree.map(lambda _: VMEM, outs),
        scratch_shapes=list(scratch),
        compiler_params=pltpu.CompilerParams(vmem_limit_bytes=VMEM_BYTES),
        cost_estimate=pl.CostEstimate(flops=flops, bytes_accessed=moved, transcendentals=0),
    )(*args)


def array(*dims):
    return jax.ShapeDtypeStruct(dims, BF16)


def pack_fields(b_ref, cols_ref, rows_ref):
    for c in range(2):
        for y in range(Y):
            cols_ref[y, c] = b_ref[c, 0, :, y * COLS : y * COLS + COLS]
        for d in range(GROUP):
            parts = [b_ref[c, 1, :, zh * 512 + d * 64 : zh * 512 + d * 64 + 64] for zh in range(ZH)]
            rows_ref[d, c] = jnp.concatenate(parts, axis=-1)


def repeat_fields(cols_ref, rows_ref, out_ref):
    for d in range(GROUP):
        for y in range(Y):
            for c in range(2):
                out_ref[d, y * 2 + c] = cols_ref[y, c]
        for c in range(2):
            out_ref[d, 2 * Y + c] = rows_ref[d, c]


def pack_matrices(diag_ref, coup_ref, out_ref):
    for c in range(2):
        out_ref[0, c] = diag_ref[c, 0]
        out_ref[1, c] = coup_ref[c]
        out_ref[2, c] = diag_ref[c, 1]


def split_matrices(m0_ref, m1_ref, m2_ref, m3_ref, first_ref, rest_ref):
    for back, ref in enumerate((m0_ref, m1_ref, m2_ref, m3_ref)):
        for c in range(2):
            first_ref[back, c] = ref[0, c]
            rest_ref[back, 0, c] = ref[1, c]
            rest_ref[back, 1, c] = ref[2, c]


def row_of(zh, back, c):
    return pl.multiple_of(c * ROWS + lax.rem(zh - back + ZH, ZH) * 64, 64)


def complex_parts(prod):
    shots, rows = prod.shape[0] // 2, prod.shape[1] // 2
    real = prod[:shots, :rows] - prod[shots:, rows:]
    imag = prod[:shots, rows:] + prod[shots:, :rows]
    return real, imag


def first_partial(at_ref, v_ref, own_ref, other_ref, out_ref, slice_ref, mat_ref, vec_ref):
    core, zh = at_ref[0], at_ref[1]
    for ref, who in ((own_ref, core), (other_ref, 1 - core)):
        col = pl.multiple_of(who * 128, 128)
        for c in range(2):
            for back in range(ZH):
                mat_ref[pl.ds(row_of(zh, back, c), 64), pl.ds(col, 128)] = ref[back, c]
    for c in range(2):
        for y in range(Y):
            row = (c * Y + y) * GROUP_SHOTS
            block = v_ref[:, y * 2 + c].reshape(GROUP_SHOTS, COLS)
            vec_ref[row : row + GROUP_SHOTS, :] = block
        slice_ref[c] = v_ref[:, 2 * Y + c].reshape(GROUP_SHOTS, ROWS)
    prod = lax.dot_general(vec_ref[...], mat_ref[...], NT, preferred_element_type=F32)
    for c, part in enumerate(complex_parts(prod)):
        out_ref[:, c] = part.reshape(Y, GROUP_SHOTS, ROWS).astype(BF16)


def first_sum(parts_ref, rep_ref, first_ref):
    for c in range(2):
        total = parts_ref[0, c].astype(F32)
        for y in range(1, Y):
            total = total + parts_ref[y, c].astype(F32)
        total = total.astype(BF16)
        first_ref[c] = total
        for d in range(GROUP):
            rep_ref[d, c] = total


def product(at_ref, v_ref, m_ref, which, mat_ref, vec_ref):
    zh = at_ref[1]
    for y in range(Y):
        for core in range(CORES):
            col = (y * CORES + core) * 128
            for back in range(ZH):
                for c in range(2):
                    mat_ref[pl.ds(row_of(zh, back, c), 64), col : col + 128] = m_ref[
                        y * CORES + core, back, which, c
                    ]
    for c in range(2):
        for h in range(ZH):
            for d in range(0, GROUP, 2):
                pair = [v_ref[d + k, c, :, h * 64 : h * 64 + 64] for k in range(2)]
                col = h * 512 + d * 64
                rows = slice(c * GROUP_SHOTS, (c + 1) * GROUP_SHOTS)
                vec_ref[rows, col : col + 128] = jnp.concatenate(pair, axis=-1)
    prod = lax.dot_general(vec_ref[...], mat_ref[...], NT, preferred_element_type=F32)
    return complex_parts(prod)


def second_stage(at_ref, v_ref, m_ref, slice_ref, rep_ref, mat_ref, vec_ref):
    for c, part in enumerate(product(at_ref, v_ref, m_ref, 0, mat_ref, vec_ref)):
        residual = (slice_ref[c].astype(F32) - part).astype(BF16)
        for d in range(GROUP):
            rep_ref[d, c] = residual


def third_stage(at_ref, v_ref, m_ref, first_ref, out_ref, mat_ref, vec_ref):
    for c, part in enumerate(product(at_ref, v_ref, m_ref, 1, mat_ref, vec_ref)):
        out_ref[:, c, 0] = first_ref[c].reshape(GROUP, SHOTS, ROWS)
        out_ref[:, c, 1] = part.reshape(GROUP, SHOTS, ROWS).astype(BF16)


def unpack(in_ref, out_ref):
    for c in range(2):
        for p in range(2):
            for h in range(ZH):
                for d in range(0, GROUP, 2):
                    pair = [in_ref[d + k, c, p, :, h * 64 : h * 64 + 64] for k in range(2)]
                    col = h * 512 + d * 64
                    out_ref[c, p, :, col : col + 128] = jnp.concatenate(pair, axis=-1)


def exchange(block, axes):
    return lax.all_to_all(block, axes, 0, 0, tiled=True)


def shift(block, axis, size, by):
    return lax.ppermute(block, axis, [(i, (i + by) % size) for i in range(size)])


def on_device(shot_fields, diag_inverse, coupling):
    group = ("zl", "x")
    at = jnp.stack([lax.axis_index("core"), lax.axis_index("zh")])

    mats = call(pack_matrices, array(3, 2, 64, 128), diag_inverse, coupling)
    mats = [mats] + [shift(mats, "zh", ZH, by) for by in range(1, ZH)]
    first_mat, rest = call(
        split_matrices, (array(ZH, 2, 64, 128), array(ZH, 2, 2, 64, 128)), *mats
    )
    rest = lax.all_gather(rest, ("y", "core"), axis=0)
    first_mat = (first_mat, shift(first_mat, "core", CORES, 1))

    cols, rows = call(
        pack_fields, (array(Y, 2, SHOTS, COLS), array(GROUP, 2, SHOTS, ROWS)), shot_fields
    )
    cols = exchange(cols, "y")
    fields = call(repeat_fields, array(GROUP, 2 * Y + 2, SHOTS, COLS), cols, rows)
    fields = exchange(fields, group)

    block = array(2, GROUP_SHOTS, ROWS)
    repeated = array(GROUP, 2, GROUP_SHOTS, ROWS)
    parts, second_slice = call(
        first_partial,
        (array(Y, 2, GROUP_SHOTS, ROWS), block),
        at,
        fields,
        *first_mat,
        scalars=1,
        scratch=[pltpu.VMEM((2 * ROWS, COLS), BF16), pltpu.VMEM((2 * Y * GROUP_SHOTS, COLS), BF16)],
    )
    first_rep, first = call(first_sum, (repeated, block), exchange(parts, "y"))

    def stage(body, outs, *args):
        scratch = [pltpu.VMEM((2 * ROWS, PANEL), BF16), pltpu.VMEM((2 * GROUP_SHOTS, PANEL), BF16)]
        flops = 2 * 2 * ROWS * PANEL * 2 * GROUP_SHOTS
        return call(body, outs, at, *args, scalars=1, scratch=scratch, flops=flops, moved=3 << 20)

    residual = stage(second_stage, repeated, exchange(first_rep, group), rest, second_slice)
    both = stage(
        third_stage, array(GROUP, 2, 2, SHOTS, ROWS), exchange(residual, group), rest, first
    )
    return call(unpack, array(2, 2, SHOTS, PANEL), exchange(both, group))


def solution(mesh):
    axes = ("zh", "zl", "x", "y", "core")
    fine = Mesh(mesh.devices.reshape(ZH, ZL, X, Y, CORES), axes)
    row, src = axes[:3], axes[3:]
    in_specs = (
        P(None, None, row + src, None),
        P(None, None, row, src),
        P(None, row, src),
    )
    out_specs = P(None, None, row + src, None)
    return jax.shard_map(
        on_device, mesh=fine, in_specs=in_specs, out_specs=out_specs, check_vma=False
    )
```

```python
import jax
import jax.numpy as jnp
from jax import lax
from jax.experimental import pallas as pl
from jax.experimental.pallas import tpu as pltpu
from jax.sharding import Mesh, PartitionSpec as P

F32, BF16 = jnp.float32, jnp.bfloat16
ZH, ZL, X, Y, CORES = 4, 2, 4, 8, 2
GROUP = ZL * X
PANEL, SHOTS = 2048, 8
ROWS = PANEL // GROUP
COLS = PANEL // Y
GROUP_SHOTS = GROUP * SHOTS
VMEM_BYTES = 40 * 1024 * 1024
VMEM = pl.BlockSpec(memory_space=pltpu.VMEM)
SMEM = pl.BlockSpec(memory_space=pltpu.SMEM)
NT = (((1,), (1,)), ((), ()))


def call(body, outs, *args, scalars=0, scratch=(), flops=0, moved=1 << 20):
    return pl.pallas_call(
        body,
        out_shape=outs,
        in_specs=[SMEM] * scalars + [VMEM] * (len(args) - scalars),
        out_specs=jax.tree.map(lambda _: VMEM, outs),
        scratch_shapes=list(scratch),
        compiler_params=pltpu.CompilerParams(vmem_limit_bytes=VMEM_BYTES),
        cost_estimate=pl.CostEstimate(flops=flops, bytes_accessed=moved, transcendentals=0),
    )(*args)


def array(*dims):
    return jax.ShapeDtypeStruct(dims, BF16)


def pack_fields(b_ref, cols_ref, rows_ref):
    for c in range(2):
        for y in range(Y):
            cols_ref[y, c] = b_ref[c, 0, :, y * COLS : y * COLS + COLS]
        for d in range(GROUP):
            parts = [b_ref[c, 1, :, zh * 512 + d * 64 : zh * 512 + d * 64 + 64] for zh in range(ZH)]
            rows_ref[d, c] = jnp.concatenate(parts, axis=-1)


def repeat_fields(cols_ref, rows_ref, out_ref):
    for d in range(GROUP):
        for y in range(Y):
            for c in range(2):
                out_ref[d, y * 2 + c] = cols_ref[y, c]
        for c in range(2):
            out_ref[d, 2 * Y + c] = rows_ref[d, c]


def pack_matrices(diag_ref, coup_ref, out_ref):
    for c in range(2):
        out_ref[0, c] = diag_ref[c, 0]
        out_ref[1, c] = coup_ref[c]
        out_ref[2, c] = diag_ref[c, 1]


def split_matrices(m0_ref, m1_ref, m2_ref, m3_ref, first_ref, rest_ref):
    for back, ref in enumerate((m0_ref, m1_ref, m2_ref, m3_ref)):
        for c in range(2):
            first_ref[back, c] = ref[0, c]
            rest_ref[back, 0, c] = ref[1, c]
            rest_ref[back, 1, c] = ref[2, c]


def row_of(zh, back, c):
    return pl.multiple_of(c * ROWS + lax.rem(zh - back + ZH, ZH) * 64, 64)


def complex_parts(prod):
    shots, rows = prod.shape[0] // 2, prod.shape[1] // 2
    real = prod[:shots, :rows] - prod[shots:, rows:]
    imag = prod[:shots, rows:] + prod[shots:, :rows]
    return real, imag


def first_partial(at_ref, v_ref, own_ref, other_ref, out_ref, slice_ref, mat_ref, vec_ref):
    core, zh = at_ref[0], at_ref[1]
    for ref, who in ((own_ref, core), (other_ref, 1 - core)):
        col = pl.multiple_of(who * 128, 128)
        for c in range(2):
            for back in range(ZH):
                mat_ref[pl.ds(row_of(zh, back, c), 64), pl.ds(col, 128)] = ref[back, c]
    for c in range(2):
        for y in range(Y):
            row = (c * Y + y) * GROUP_SHOTS
            block = v_ref[:, y * 2 + c].reshape(GROUP_SHOTS, COLS)
            vec_ref[row : row + GROUP_SHOTS, :] = block
        slice_ref[c] = v_ref[:, 2 * Y + c].reshape(GROUP_SHOTS, ROWS)
    prod = lax.dot_general(vec_ref[...], mat_ref[...], NT, preferred_element_type=F32)
    for c, part in enumerate(complex_parts(prod)):
        out_ref[:, c] = part.reshape(Y, GROUP_SHOTS, ROWS).astype(BF16)


def first_sum(parts_ref, rep_ref, first_ref):
    for c in range(2):
        total = parts_ref[0, c].astype(F32)
        for y in range(1, Y):
            total = total + parts_ref[y, c].astype(F32)
        total = total.astype(BF16)
        first_ref[c] = total
        for d in range(GROUP):
            rep_ref[d, c] = total


def product(at_ref, v_ref, m_ref, which, mat_ref, vec_ref):
    zh = at_ref[1]
    for y in range(Y):
        for core in range(CORES):
            col = (y * CORES + core) * 128
            for back in range(ZH):
                for c in range(2):
                    mat_ref[pl.ds(row_of(zh, back, c), 64), col : col + 128] = m_ref[
                        y * CORES + core, back, which, c
                    ]
    for c in range(2):
        for h in range(ZH):
            for d in range(0, GROUP, 2):
                pair = [v_ref[d + k, c, :, h * 64 : h * 64 + 64] for k in range(2)]
                col = h * 512 + d * 64
                rows = slice(c * GROUP_SHOTS, (c + 1) * GROUP_SHOTS)
                vec_ref[rows, col : col + 128] = jnp.concatenate(pair, axis=-1)
    prod = lax.dot_general(vec_ref[...], mat_ref[...], NT, preferred_element_type=F32)
    return complex_parts(prod)


def second_stage(at_ref, v_ref, m_ref, slice_ref, rep_ref, mat_ref, vec_ref):
    for c, part in enumerate(product(at_ref, v_ref, m_ref, 0, mat_ref, vec_ref)):
        residual = (slice_ref[c].astype(F32) - part).astype(BF16)
        for d in range(GROUP):
            rep_ref[d, c] = residual


def third_stage(at_ref, v_ref, m_ref, first_ref, out_ref, mat_ref, vec_ref):
    for c, part in enumerate(product(at_ref, v_ref, m_ref, 1, mat_ref, vec_ref)):
        out_ref[:, c, 0] = first_ref[c].reshape(GROUP, SHOTS, ROWS)
        out_ref[:, c, 1] = part.reshape(GROUP, SHOTS, ROWS).astype(BF16)


def unpack(in_ref, out_ref):
    for c in range(2):
        for p in range(2):
            for h in range(ZH):
                for d in range(0, GROUP, 2):
                    pair = [in_ref[d + k, c, p, :, h * 64 : h * 64 + 64] for k in range(2)]
                    col = h * 512 + d * 64
                    out_ref[c, p, :, col : col + 128] = jnp.concatenate(pair, axis=-1)


def exchange(block, axes):
    return lax.all_to_all(block, axes, 0, 0, tiled=True)


def shift(block, axis, size, by):
    return lax.ppermute(block, axis, [(i, (i + by) % size) for i in range(size)])


def on_device(shot_fields, diag_inverse, coupling):
    group = ("zl", "x")
    at = jnp.stack([lax.axis_index("core"), lax.axis_index("zh")])

    cols, rows = call(
        pack_fields, (array(Y, 2, SHOTS, COLS), array(GROUP, 2, SHOTS, ROWS)), shot_fields
    )
    mats = call(pack_matrices, array(3, 2, 64, 128), diag_inverse, coupling)
    cols, mats = lax.optimization_barrier((cols, mats))
    moved = [shift(mats, "zh", ZH, by) for by in range(1, ZH)]
    cols, *moved = lax.optimization_barrier((exchange(cols, "y"), *moved))
    first_mat, rest = call(
        split_matrices, (array(ZH, 2, 64, 128), array(ZH, 2, 2, 64, 128)), mats, *moved
    )
    rest = lax.all_gather(rest, ("y", "core"), axis=0)
    first_mat = (first_mat, shift(first_mat, "core", CORES, 1))
    fields = call(repeat_fields, array(GROUP, 2 * Y + 2, SHOTS, COLS), cols, rows)
    fields = exchange(fields, group)

    block = array(2, GROUP_SHOTS, ROWS)
    repeated = array(GROUP, 2, GROUP_SHOTS, ROWS)
    parts, second_slice = call(
        first_partial,
        (array(Y, 2, GROUP_SHOTS, ROWS), block),
        at,
        fields,
        *first_mat,
        scalars=1,
        scratch=[pltpu.VMEM((2 * ROWS, COLS), BF16), pltpu.VMEM((2 * Y * GROUP_SHOTS, COLS), BF16)],
    )
    first_rep, first = call(first_sum, (repeated, block), exchange(parts, "y"))

    def stage(body, outs, *args):
        scratch = [pltpu.VMEM((2 * ROWS, PANEL), BF16), pltpu.VMEM((2 * GROUP_SHOTS, PANEL), BF16)]
        flops = 2 * 2 * ROWS * PANEL * 2 * GROUP_SHOTS
        return call(body, outs, at, *args, scalars=1, scratch=scratch, flops=flops, moved=3 << 20)

    residual = stage(second_stage, repeated, exchange(first_rep, group), rest, second_slice)
    both = stage(
        third_stage, array(GROUP, 2, 2, SHOTS, ROWS), exchange(residual, group), rest, first
    )
    return call(unpack, array(2, 2, SHOTS, PANEL), exchange(both, group))


def solution(mesh):
    axes = ("zh", "zl", "x", "y", "core")
    fine = Mesh(mesh.devices.reshape(ZH, ZL, X, Y, CORES), axes)
    row, src = axes[:3], axes[3:]
    in_specs = (
        P(None, None, row + src, None),
        P(None, None, row, src),
        P(None, row, src),
    )
    out_specs = P(None, None, row + src, None)
    return jax.shard_map(
        on_device, mesh=fine, in_specs=in_specs, out_specs=out_specs, check_vma=False
    )
```

```python
import jax
import jax.numpy as jnp
from jax import lax
from jax.experimental import pallas as pl
from jax.experimental.pallas import tpu as pltpu
from jax.sharding import Mesh, PartitionSpec as P

F32, BF16 = jnp.float32, jnp.bfloat16
ZH, ZL, X, Y, CORES = 4, 2, 4, 8, 2
SRC = Y * CORES
GROUP = ZL * X
PANEL, SHOTS = 2048, 8
ROWS = PANEL // GROUP
GROUP_SHOTS = GROUP * SHOTS
VMEM_BYTES = 40 * 1024 * 1024
VMEM = pl.BlockSpec(memory_space=pltpu.VMEM)
NT = (((1,), (1,)), ((), ()))


def call(body, outs, *args, scratch=(), flops=0, moved=1 << 20):
    return pl.pallas_call(
        body,
        out_shape=outs,
        in_specs=[VMEM] * len(args),
        out_specs=jax.tree.map(lambda _: VMEM, outs),
        scratch_shapes=list(scratch),
        compiler_params=pltpu.CompilerParams(vmem_limit_bytes=VMEM_BYTES),
        cost_estimate=pl.CostEstimate(flops=flops, bytes_accessed=moved, transcendentals=0),
    )(*args)


def array(*dims):
    return jax.ShapeDtypeStruct(dims, BF16)


def pack(b_ref, out_ref):
    for c in range(2):
        for d in range(GROUP):
            out_ref[d, c, :, 0:PANEL] = b_ref[c, 0]
            parts = [b_ref[c, 1, :, zh * 512 + d * 64 : zh * 512 + d * 64 + 64] for zh in range(ZH)]
            out_ref[d, c, :, PANEL : PANEL + ROWS] = jnp.concatenate(parts, axis=-1)


def complex_parts(prod):
    shots, rows = prod.shape[0] // 2, prod.shape[1] // 2
    real = prod[:shots, :rows] - prod[shots:, rows:]
    imag = prod[:shots, rows:] + prod[shots:, :rows]
    return real, imag


def place_matrix(which, m_ref, mat_ref):
    for src in range(SRC):
        for zh in range(ZH):
            for c in range(2):
                row, col = c * ROWS + zh * 64, src * 128
                mat_ref[row : row + 64, col : col + 128] = m_ref[src, zh, which, c]


def product(v_ref, mat_ref, vec_ref):
    for c in range(2):
        for h in range(ZH):
            for d in range(0, GROUP, 2):
                pair = [v_ref[d + k, c, :, h * 64 : h * 64 + 64] for k in range(2)]
                col = h * 512 + d * 64
                rows = slice(c * GROUP_SHOTS, (c + 1) * GROUP_SHOTS)
                vec_ref[rows, col : col + 128] = jnp.concatenate(pair, axis=-1)
    prod = lax.dot_general(vec_ref[...], mat_ref[...], NT, preferred_element_type=F32)
    return complex_parts(prod)


def first_stage(v_ref, m_ref, rep_ref, first_ref, slice_ref, mat_ref, vec_ref):
    place_matrix(0, m_ref, mat_ref)
    for c in range(2):
        rows = slice(c * GROUP_SHOTS, (c + 1) * GROUP_SHOTS)
        vec_ref[rows, :] = v_ref[:, c, :, 0:PANEL].reshape(GROUP_SHOTS, PANEL)
        slice_ref[c] = v_ref[:, c, :, PANEL : PANEL + ROWS].reshape(GROUP_SHOTS, ROWS)
    prod = lax.dot_general(vec_ref[...], mat_ref[...], NT, preferred_element_type=F32)
    for c, part in enumerate(complex_parts(prod)):
        part = part.astype(BF16)
        first_ref[c] = part
        for d in range(GROUP):
            rep_ref[d, c] = part


def second_stage(v_ref, m_ref, slice_ref, rep_ref, mat_ref, vec_ref):
    place_matrix(1, m_ref, mat_ref)
    for c, part in enumerate(product(v_ref, mat_ref, vec_ref)):
        residual = (slice_ref[c].astype(F32) - part).astype(BF16)
        for d in range(GROUP):
            rep_ref[d, c] = residual


def third_stage(v_ref, m_ref, first_ref, out_ref, mat_ref, vec_ref):
    place_matrix(2, m_ref, mat_ref)
    for c, part in enumerate(product(v_ref, mat_ref, vec_ref)):
        out_ref[:, c, 0] = first_ref[c].reshape(GROUP, SHOTS, ROWS)
        out_ref[:, c, 1] = part.reshape(GROUP, SHOTS, ROWS).astype(BF16)


def unpack(in_ref, out_ref):
    for c in range(2):
        for p in range(2):
            for h in range(ZH):
                for d in range(0, GROUP, 2):
                    pair = [in_ref[d + k, c, p, :, h * 64 : h * 64 + 64] for k in range(2)]
                    col = h * 512 + d * 64
                    out_ref[c, p, :, col : col + 128] = jnp.concatenate(pair, axis=-1)


def exchange(block, axes):
    return lax.all_to_all(block, axes, 0, 0, tiled=True)


def on_device(shot_fields, diag_inverse, coupling):
    group = ("zl", "x")
    block = array(2, GROUP_SHOTS, ROWS)
    repeated = array(GROUP, 2, GROUP_SHOTS, ROWS)

    mats = jnp.stack([diag_inverse[:, 0], coupling, diag_inverse[:, 1]])
    mats = lax.all_gather(mats, "zh", axis=0)
    mats = lax.all_gather(mats, ("y", "core"), axis=0)
    fields = call(pack, array(GROUP, 2, SHOTS, PANEL + ROWS), shot_fields)

    def stage(body, outs, sent, *args):
        scratch = [pltpu.VMEM((2 * ROWS, PANEL), BF16), pltpu.VMEM((2 * GROUP_SHOTS, PANEL), BF16)]
        flops = 2 * 2 * ROWS * PANEL * 2 * GROUP_SHOTS
        fields = exchange(sent, group)
        return call(body, outs, fields, mats, *args, scratch=scratch, flops=flops, moved=3 << 20)

    first_rep, first, second_slice = stage(first_stage, (repeated, block, block), fields)
    residual = stage(second_stage, repeated, first_rep, second_slice)
    both = stage(third_stage, array(GROUP, 2, 2, SHOTS, ROWS), residual, first)
    return call(unpack, array(2, 2, SHOTS, PANEL), exchange(both, group))


def solution(mesh):
    axes = ("zh", "zl", "x", "y", "core")
    fine = Mesh(mesh.devices.reshape(ZH, ZL, X, Y, CORES), axes)
    row, src = axes[:3], axes[3:]
    in_specs = (
        P(None, None, row + src, None),
        P(None, None, row, src),
        P(None, row, src),
    )
    out_specs = P(None, None, row + src, None)
    return jax.shard_map(
        on_device, mesh=fine, in_specs=in_specs, out_specs=out_specs, check_vma=False
    )
```

```python
import jax
import jax.numpy as jnp
from jax import lax
from jax.experimental import pallas as pl
from jax.experimental.pallas import tpu as pltpu
from jax.sharding import Mesh, PartitionSpec as P

F32, BF16 = jnp.float32, jnp.bfloat16
ZH, ZL, X, Y, CORES = 4, 2, 4, 8, 2
SRC = Y * CORES
GROUP = ZL * X
PANEL, SHOTS = 2048, 8
ROWS = PANEL // GROUP
GROUP_SHOTS = GROUP * SHOTS
VMEM_BYTES = 40 * 1024 * 1024
VMEM = pl.BlockSpec(memory_space=pltpu.VMEM)
FIRST, SECOND, COUPLING = (0, 2), (1, 3), (4, 5)
NT = (((1,), (1,)), ((), ()))


def call(body, outs, *args, scratch=(), flops=0, moved=1 << 20):
    return pl.pallas_call(
        body,
        out_shape=outs,
        in_specs=[VMEM] * len(args),
        out_specs=jax.tree.map(lambda _: VMEM, outs),
        scratch_shapes=list(scratch),
        compiler_params=pltpu.CompilerParams(vmem_limit_bytes=VMEM_BYTES),
        cost_estimate=pl.CostEstimate(flops=flops, bytes_accessed=moved, transcendentals=0),
    )(*args)


def array(*dims):
    return jax.ShapeDtypeStruct(dims, BF16)


def pack(b_ref, out_ref):
    for c in range(2):
        for d in range(GROUP):
            out_ref[d, c, :, 0:PANEL] = b_ref[c, 0]
            parts = [b_ref[c, 1, :, zh * 512 + d * 64 : zh * 512 + d * 64 + 64] for zh in range(ZH)]
            out_ref[d, c, :, PANEL : PANEL + ROWS] = jnp.concatenate(parts, axis=-1)


def complex_parts(prod):
    shots, rows = prod.shape[0] // 2, prod.shape[1] // 2
    real = prod[:shots, :rows] - prod[shots:, rows:]
    imag = prod[:shots, rows:] + prod[shots:, :rows]
    return real, imag


def place_matrix(pair, m_ref, mat_ref):
    for src in range(SRC):
        for zh in range(ZH):
            for c in range(2):
                row, col = c * ROWS + zh * 64, src * 128
                mat_ref[row : row + 64, col : col + 128] = m_ref[src, zh, pair[c]]


def product(v_ref, mat_ref, vec_ref):
    for c in range(2):
        for h in range(ZH):
            for d in range(0, GROUP, 2):
                pair = [v_ref[d + k, c, :, h * 64 : h * 64 + 64] for k in range(2)]
                col = h * 512 + d * 64
                rows = slice(c * GROUP_SHOTS, (c + 1) * GROUP_SHOTS)
                vec_ref[rows, col : col + 128] = jnp.concatenate(pair, axis=-1)
    prod = lax.dot_general(vec_ref[...], mat_ref[...], NT, preferred_element_type=F32)
    return complex_parts(prod)


def first_stage(v_ref, m_ref, rep_ref, first_ref, slice_ref, mat_ref, vec_ref):
    place_matrix(FIRST, m_ref, mat_ref)
    for c in range(2):
        rows = slice(c * GROUP_SHOTS, (c + 1) * GROUP_SHOTS)
        vec_ref[rows, :] = v_ref[:, c, :, 0:PANEL].reshape(GROUP_SHOTS, PANEL)
        slice_ref[c] = v_ref[:, c, :, PANEL : PANEL + ROWS].reshape(GROUP_SHOTS, ROWS)
    prod = lax.dot_general(vec_ref[...], mat_ref[...], NT, preferred_element_type=F32)
    for c, part in enumerate(complex_parts(prod)):
        part = part.astype(BF16)
        first_ref[c] = part
        for d in range(GROUP):
            rep_ref[d, c] = part


def second_stage(v_ref, m_ref, slice_ref, rep_ref, mat_ref, vec_ref):
    place_matrix(COUPLING, m_ref, mat_ref)
    for c, part in enumerate(product(v_ref, mat_ref, vec_ref)):
        residual = (slice_ref[c].astype(F32) - part).astype(BF16)
        for d in range(GROUP):
            rep_ref[d, c] = residual


def third_stage(v_ref, m_ref, first_ref, out_ref, mat_ref, vec_ref):
    place_matrix(SECOND, m_ref, mat_ref)
    for c, part in enumerate(product(v_ref, mat_ref, vec_ref)):
        out_ref[:, c, 0] = first_ref[c].reshape(GROUP, SHOTS, ROWS)
        out_ref[:, c, 1] = part.reshape(GROUP, SHOTS, ROWS).astype(BF16)


def unpack(in_ref, out_ref):
    for c in range(2):
        for p in range(2):
            for h in range(ZH):
                for d in range(0, GROUP, 2):
                    pair = [in_ref[d + k, c, p, :, h * 64 : h * 64 + 64] for k in range(2)]
                    col = h * 512 + d * 64
                    out_ref[c, p, :, col : col + 128] = jnp.concatenate(pair, axis=-1)


def exchange(block, axes):
    return lax.all_to_all(block, axes, 0, 0, tiled=True)


def on_device(shot_fields, diag_inverse, coupling):
    group = ("zl", "x")
    block = array(2, GROUP_SHOTS, ROWS)
    repeated = array(GROUP, 2, GROUP_SHOTS, ROWS)

    mats = jnp.concatenate([diag_inverse.reshape(4, 64, 128), coupling])
    mats = lax.all_gather(mats, "zh", axis=0)
    mats = lax.all_gather(mats, ("y", "core"), axis=0)
    fields = call(pack, array(GROUP, 2, SHOTS, PANEL + ROWS), shot_fields)

    def stage(body, outs, sent, *args):
        scratch = [pltpu.VMEM((2 * ROWS, PANEL), BF16), pltpu.VMEM((2 * GROUP_SHOTS, PANEL), BF16)]
        flops = 2 * 2 * ROWS * PANEL * 2 * GROUP_SHOTS
        fields = exchange(sent, group)
        return call(body, outs, fields, mats, *args, scratch=scratch, flops=flops, moved=3 << 20)

    first_rep, first, second_slice = stage(first_stage, (repeated, block, block), fields)
    residual = stage(second_stage, repeated, first_rep, second_slice)
    both = stage(third_stage, array(GROUP, 2, 2, SHOTS, ROWS), residual, first)
    return call(unpack, array(2, 2, SHOTS, PANEL), exchange(both, group))


def solution(mesh):
    axes = ("zh", "zl", "x", "y", "core")
    fine = Mesh(mesh.devices.reshape(ZH, ZL, X, Y, CORES), axes)
    row, src = axes[:3], axes[3:]
    in_specs = (
        P(None, None, row + src, None),
        P(None, None, row, src),
        P(None, row, src),
    )
    out_specs = P(None, None, row + src, None)
    return jax.shard_map(
        on_device, mesh=fine, in_specs=in_specs, out_specs=out_specs, check_vma=False
    )
```

```python
import jax
import jax.numpy as jnp
from jax import lax
from jax.experimental import pallas as pl
from jax.experimental.pallas import tpu as pltpu
from jax.sharding import Mesh, PartitionSpec as P

F32, BF16 = jnp.float32, jnp.bfloat16
ZH, ZL, X, Y, CORES = 4, 2, 4, 8, 2
SRC = Y * CORES
GROUP = ZL * X
PANEL, SHOTS = 2048, 8
ROWS = PANEL // GROUP
GROUP_SHOTS = GROUP * SHOTS
VMEM_BYTES = 40 * 1024 * 1024
VMEM = pl.BlockSpec(memory_space=pltpu.VMEM)
FIRST, SECOND, COUPLING = (0, 2), (1, 3), (4, 5)
NT = (((1,), (1,)), ((), ()))


def call(body, outs, *args, scratch=(), flops=0, moved=1 << 20):
    return pl.pallas_call(
        body,
        out_shape=outs,
        in_specs=[VMEM] * len(args),
        out_specs=jax.tree.map(lambda _: VMEM, outs),
        scratch_shapes=list(scratch),
        compiler_params=pltpu.CompilerParams(vmem_limit_bytes=VMEM_BYTES),
        cost_estimate=pl.CostEstimate(flops=flops, bytes_accessed=moved, transcendentals=0),
    )(*args)


def array(*dims):
    return jax.ShapeDtypeStruct(dims, BF16)


def pack(b_ref, out_ref):
    for c in range(2):
        for d in range(GROUP):
            out_ref[d, c, :, 0:PANEL] = b_ref[c, 0]
            parts = [b_ref[c, 1, :, zh * 512 + d * 64 : zh * 512 + d * 64 + 64] for zh in range(ZH)]
            out_ref[d, c, :, PANEL : PANEL + ROWS] = jnp.concatenate(parts, axis=-1)


def complex_parts(prod):
    shots, rows = prod.shape[0] // 2, prod.shape[1] // 2
    real = prod[:shots, :rows] - prod[shots:, rows:]
    imag = prod[:shots, rows:] + prod[shots:, :rows]
    return real, imag


def place_matrix(pair, m_ref, mat_ref):
    for src in range(SRC):
        for zh in range(ZH):
            for c in range(2):
                row, col = c * ROWS + zh * 64, src * 128
                mat_ref[row : row + 64, col : col + 128] = m_ref[src, zh, pair[c]]


def product(v_ref, mat_ref, vec_ref):
    for c in range(2):
        for h in range(ZH):
            for d in range(0, GROUP, 2):
                pair = [v_ref[d + k, c, :, h * 64 : h * 64 + 64] for k in range(2)]
                col = h * 512 + d * 64
                rows = slice(c * GROUP_SHOTS, (c + 1) * GROUP_SHOTS)
                vec_ref[rows, col : col + 128] = jnp.concatenate(pair, axis=-1)
    prod = lax.dot_general(vec_ref[...], mat_ref[...], NT, preferred_element_type=F32)
    return complex_parts(prod)


def place_fields(v_ref, vec_ref, slice_ref):
    for c in range(2):
        rows = slice(c * GROUP_SHOTS, (c + 1) * GROUP_SHOTS)
        vec_ref[rows, :] = v_ref[:, c, :, 0:PANEL].reshape(GROUP_SHOTS, PANEL)
        slice_ref[c] = v_ref[:, c, :, PANEL : PANEL + ROWS].reshape(GROUP_SHOTS, ROWS)


def first_stage(vec_ref, m_ref, rep_ref, first_ref, mat_ref):
    place_matrix(FIRST, m_ref, mat_ref)
    prod = lax.dot_general(vec_ref[...], mat_ref[...], NT, preferred_element_type=F32)
    for c, part in enumerate(complex_parts(prod)):
        part = part.astype(BF16)
        first_ref[c] = part
        for d in range(GROUP):
            rep_ref[d, c] = part


def second_stage(v_ref, m_ref, slice_ref, rep_ref, mat_ref, vec_ref):
    place_matrix(COUPLING, m_ref, mat_ref)
    for c, part in enumerate(product(v_ref, mat_ref, vec_ref)):
        residual = (slice_ref[c].astype(F32) - part).astype(BF16)
        for d in range(GROUP):
            rep_ref[d, c] = residual


def third_stage(v_ref, m_ref, first_ref, out_ref, mat_ref, vec_ref):
    place_matrix(SECOND, m_ref, mat_ref)
    for c, part in enumerate(product(v_ref, mat_ref, vec_ref)):
        out_ref[:, c, 0] = first_ref[c].reshape(GROUP, SHOTS, ROWS)
        out_ref[:, c, 1] = part.reshape(GROUP, SHOTS, ROWS).astype(BF16)


def unpack(in_ref, out_ref):
    for c in range(2):
        for p in range(2):
            for h in range(ZH):
                for d in range(0, GROUP, 2):
                    pair = [in_ref[d + k, c, p, :, h * 64 : h * 64 + 64] for k in range(2)]
                    col = h * 512 + d * 64
                    out_ref[c, p, :, col : col + 128] = jnp.concatenate(pair, axis=-1)


def exchange(block, axes):
    return lax.all_to_all(block, axes, 0, 0, tiled=True)


def on_device(shot_fields, diag_inverse, coupling):
    group = ("zl", "x")
    block = array(2, GROUP_SHOTS, ROWS)
    repeated = array(GROUP, 2, GROUP_SHOTS, ROWS)

    mats = jnp.concatenate([diag_inverse.reshape(4, 64, 128), coupling])
    mats = lax.all_gather(mats, "zh", axis=0)
    mats = lax.all_gather(mats, ("y", "core"), axis=0)
    fields = call(pack, array(GROUP, 2, SHOTS, PANEL + ROWS), shot_fields)

    flops = 2 * 2 * ROWS * PANEL * 2 * GROUP_SHOTS
    matrix, vector = pltpu.VMEM((2 * ROWS, PANEL), BF16), pltpu.VMEM((2 * GROUP_SHOTS, PANEL), BF16)

    def stage(body, outs, sent, *args):
        fields = exchange(sent, group)
        scratch = [matrix, vector]
        return call(body, outs, fields, mats, *args, scratch=scratch, flops=flops, moved=3 << 20)

    placed, second_slice = call(
        place_fields, (array(2 * GROUP_SHOTS, PANEL), block), exchange(fields, group)
    )
    first_rep, first = call(
        first_stage,
        (repeated, block),
        placed,
        mats,
        scratch=[matrix],
        flops=flops,
        moved=3 << 20,
    )
    residual = stage(second_stage, repeated, first_rep, second_slice)
    both = stage(third_stage, array(GROUP, 2, 2, SHOTS, ROWS), residual, first)
    return call(unpack, array(2, 2, SHOTS, PANEL), exchange(both, group))


def solution(mesh):
    axes = ("zh", "zl", "x", "y", "core")
    fine = Mesh(mesh.devices.reshape(ZH, ZL, X, Y, CORES), axes)
    row, src = axes[:3], axes[3:]
    in_specs = (
        P(None, None, row + src, None),
        P(None, None, row, src),
        P(None, row, src),
    )
    out_specs = P(None, None, row + src, None)
    return jax.shard_map(
        on_device, mesh=fine, in_specs=in_specs, out_specs=out_specs, check_vma=False
    )
```

```python
import jax
import jax.numpy as jnp
from jax import lax
from jax.experimental import pallas as pl
from jax.experimental.pallas import tpu as pltpu
from jax.sharding import Mesh, PartitionSpec as P

F32, BF16 = jnp.float32, jnp.bfloat16
ZH, ZL, X, Y, CORES = 4, 2, 4, 8, 2
SRC = Y * CORES
GROUP = ZL * X
PANEL, SHOTS = 2048, 8
ROWS = PANEL // GROUP
GROUP_SHOTS = GROUP * SHOTS
VMEM_BYTES = 40 * 1024 * 1024
VMEM = pl.BlockSpec(memory_space=pltpu.VMEM)
FIRST, SECOND, COUPLING = (0, 2), (1, 3), (4, 5)
NT = (((1,), (1,)), ((), ()))


def call(body, outs, *args, scratch=(), flops=0, moved=1 << 20):
    return pl.pallas_call(
        body,
        out_shape=outs,
        in_specs=[VMEM] * len(args),
        out_specs=jax.tree.map(lambda _: VMEM, outs),
        scratch_shapes=list(scratch),
        compiler_params=pltpu.CompilerParams(vmem_limit_bytes=VMEM_BYTES),
        cost_estimate=pl.CostEstimate(flops=flops, bytes_accessed=moved, transcendentals=0),
    )(*args)


def array(*dims):
    return jax.ShapeDtypeStruct(dims, BF16)


def pack(b_ref, out_ref):
    for c in range(2):
        for d in range(GROUP):
            out_ref[d, c, :, 0:PANEL] = b_ref[c, 0]
            parts = [b_ref[c, 1, :, zh * 512 + d * 64 : zh * 512 + d * 64 + 64] for zh in range(ZH)]
            out_ref[d, c, :, PANEL : PANEL + ROWS] = jnp.concatenate(parts, axis=-1)


def complex_parts(prod):
    shots, rows = prod.shape[0] // 2, prod.shape[1] // 2
    real = prod[:shots, :rows] - prod[shots:, rows:]
    imag = prod[:shots, rows:] + prod[shots:, :rows]
    return real, imag


def place_matrix(pair, m_ref, mat_ref):
    for src in range(SRC):
        for zh in range(ZH):
            for c in range(2):
                row, col = c * ROWS + zh * 64, src * 128
                mat_ref[row : row + 64, col : col + 128] = m_ref[src, zh, pair[c]]


def product(v_ref, mat_ref, vec_ref):
    for c in range(2):
        for h in range(ZH):
            for d in range(0, GROUP, 2):
                pair = [v_ref[d + k, c, :, h * 64 : h * 64 + 64] for k in range(2)]
                col = h * 512 + d * 64
                rows = slice(c * GROUP_SHOTS, (c + 1) * GROUP_SHOTS)
                vec_ref[rows, col : col + 128] = jnp.concatenate(pair, axis=-1)
    prod = lax.dot_general(vec_ref[...], mat_ref[...], NT, preferred_element_type=F32)
    return complex_parts(prod)


def first_stage(v_ref, m_ref, rep_ref, first_ref, slice_ref, mat_ref, vec_ref):
    place_matrix(FIRST, m_ref, mat_ref)
    for c in range(2):
        rows = slice(c * GROUP_SHOTS, (c + 1) * GROUP_SHOTS)
        vec_ref[rows, :] = v_ref[:, c, :, 0:PANEL].reshape(GROUP_SHOTS, PANEL)
        slice_ref[c] = v_ref[:, c, :, PANEL : PANEL + ROWS].reshape(GROUP_SHOTS, ROWS)
    prod = lax.dot_general(vec_ref[...], mat_ref[...], NT, preferred_element_type=F32)
    for c, part in enumerate(complex_parts(prod)):
        part = part.astype(BF16)
        first_ref[c] = part
        for d in range(GROUP):
            rep_ref[d, c] = part


def second_stage(v_ref, m_ref, slice_ref, rep_ref, mat_ref, vec_ref):
    place_matrix(COUPLING, m_ref, mat_ref)
    for c, part in enumerate(product(v_ref, mat_ref, vec_ref)):
        residual = (slice_ref[c].astype(F32) - part).astype(BF16)
        for d in range(GROUP):
            rep_ref[d, c] = residual


def third_stage(v_ref, m_ref, first_ref, out_ref, mat_ref, vec_ref):
    place_matrix(SECOND, m_ref, mat_ref)
    for c, part in enumerate(product(v_ref, mat_ref, vec_ref)):
        out_ref[:, c, 0] = first_ref[c].reshape(GROUP, SHOTS, ROWS)
        out_ref[:, c, 1] = part.reshape(GROUP, SHOTS, ROWS).astype(BF16)


def unpack(in_ref, out_ref):
    for c in range(2):
        for p in range(2):
            for h in range(ZH):
                for d in range(0, GROUP, 2):
                    pair = [in_ref[d + k, c, p, :, h * 64 : h * 64 + 64] for k in range(2)]
                    col = h * 512 + d * 64
                    out_ref[c, p, :, col : col + 128] = jnp.concatenate(pair, axis=-1)


def exchange(block, axes):
    return lax.all_to_all(block, axes, 0, 0, tiled=True)


def on_device(shot_fields, diag_inverse, coupling):
    group = ("zl", "x")
    block = array(2, GROUP_SHOTS, ROWS)
    repeated = array(GROUP, 2, GROUP_SHOTS, ROWS)

    mats = jnp.concatenate([diag_inverse.reshape(4, 64, 128), coupling])
    mats = exchange(jnp.broadcast_to(mats[None], (ZH,) + mats.shape), "zh")
    mats = lax.all_gather(mats, ("y", "core"), axis=0)
    fields = call(pack, array(GROUP, 2, SHOTS, PANEL + ROWS), shot_fields)

    def stage(body, outs, sent, *args):
        scratch = [pltpu.VMEM((2 * ROWS, PANEL), BF16), pltpu.VMEM((2 * GROUP_SHOTS, PANEL), BF16)]
        flops = 2 * 2 * ROWS * PANEL * 2 * GROUP_SHOTS
        fields = exchange(sent, group)
        return call(body, outs, fields, mats, *args, scratch=scratch, flops=flops, moved=3 << 20)

    first_rep, first, second_slice = stage(first_stage, (repeated, block, block), fields)
    residual = stage(second_stage, repeated, first_rep, second_slice)
    both = stage(third_stage, array(GROUP, 2, 2, SHOTS, ROWS), residual, first)
    return call(unpack, array(2, 2, SHOTS, PANEL), exchange(both, group))


def solution(mesh):
    axes = ("zh", "zl", "x", "y", "core")
    fine = Mesh(mesh.devices.reshape(ZH, ZL, X, Y, CORES), axes)
    row, src = axes[:3], axes[3:]
    in_specs = (
        P(None, None, row + src, None),
        P(None, None, row, src),
        P(None, row, src),
    )
    out_specs = P(None, None, row + src, None)
    return jax.shard_map(
        on_device, mesh=fine, in_specs=in_specs, out_specs=out_specs, check_vma=False
    )
```

```python
import jax
import jax.numpy as jnp
from jax import lax
from jax.experimental import pallas as pl
from jax.experimental.pallas import tpu as pltpu
from jax.sharding import Mesh, PartitionSpec as P

F32, BF16 = jnp.float32, jnp.bfloat16
ZH, ZL, X, Y, CORES = 4, 2, 4, 8, 2
SRC = Y * CORES
GROUP = ZL * X
PANEL, SHOTS = 2048, 8
ROWS = PANEL // GROUP
GROUP_SHOTS = GROUP * SHOTS
VMEM_BYTES = 16 * 1024 * 1024
VMEM = pl.BlockSpec(memory_space=pltpu.VMEM)
FIRST, SECOND, COUPLING = (0, 2), (1, 3), (4, 5)
NT = (((1,), (1,)), ((), ()))


def call(body, outs, *args, scratch=(), flops=0, moved=1 << 20):
    return pl.pallas_call(
        body,
        out_shape=outs,
        in_specs=[VMEM] * len(args),
        out_specs=jax.tree.map(lambda _: VMEM, outs),
        scratch_shapes=list(scratch),
        compiler_params=pltpu.CompilerParams(vmem_limit_bytes=VMEM_BYTES),
        cost_estimate=pl.CostEstimate(flops=flops, bytes_accessed=moved, transcendentals=0),
    )(*args)


def array(*dims):
    return jax.ShapeDtypeStruct(dims, BF16)


def pack(b_ref, out_ref):
    for c in range(2):
        for d in range(GROUP):
            out_ref[d, c, :, 0:PANEL] = b_ref[c, 0]
            parts = [b_ref[c, 1, :, zh * 512 + d * 64 : zh * 512 + d * 64 + 64] for zh in range(ZH)]
            out_ref[d, c, :, PANEL : PANEL + ROWS] = jnp.concatenate(parts, axis=-1)


def complex_parts(prod):
    shots, rows = prod.shape[0] // 2, prod.shape[1] // 2
    real = prod[:shots, :rows] - prod[shots:, rows:]
    imag = prod[:shots, rows:] + prod[shots:, :rows]
    return real, imag


def place_matrix(pair, m_ref, mat_ref):
    for src in range(SRC):
        for zh in range(ZH):
            for c in range(2):
                row, col = c * ROWS + zh * 64, src * 128
                mat_ref[row : row + 64, col : col + 128] = m_ref[src, zh, pair[c]]


def product(v_ref, mat_ref, vec_ref):
    for c in range(2):
        for h in range(ZH):
            for d in range(0, GROUP, 2):
                pair = [v_ref[d + k, c, :, h * 64 : h * 64 + 64] for k in range(2)]
                col = h * 512 + d * 64
                rows = slice(c * GROUP_SHOTS, (c + 1) * GROUP_SHOTS)
                vec_ref[rows, col : col + 128] = jnp.concatenate(pair, axis=-1)
    prod = lax.dot_general(vec_ref[...], mat_ref[...], NT, preferred_element_type=F32)
    return complex_parts(prod)


def first_stage(v_ref, m_ref, rep_ref, first_ref, slice_ref, mat_ref, vec_ref):
    place_matrix(FIRST, m_ref, mat_ref)
    for c in range(2):
        rows = slice(c * GROUP_SHOTS, (c + 1) * GROUP_SHOTS)
        vec_ref[rows, :] = v_ref[:, c, :, 0:PANEL].reshape(GROUP_SHOTS, PANEL)
        slice_ref[c] = v_ref[:, c, :, PANEL : PANEL + ROWS].reshape(GROUP_SHOTS, ROWS)
    prod = lax.dot_general(vec_ref[...], mat_ref[...], NT, preferred_element_type=F32)
    for c, part in enumerate(complex_parts(prod)):
        part = part.astype(BF16)
        first_ref[c] = part
        for d in range(GROUP):
            rep_ref[d, c] = part


def second_stage(v_ref, m_ref, slice_ref, rep_ref, mat_ref, vec_ref):
    place_matrix(COUPLING, m_ref, mat_ref)
    for c, part in enumerate(product(v_ref, mat_ref, vec_ref)):
        residual = (slice_ref[c].astype(F32) - part).astype(BF16)
        for d in range(GROUP):
            rep_ref[d, c] = residual


def third_stage(v_ref, m_ref, first_ref, out_ref, mat_ref, vec_ref):
    place_matrix(SECOND, m_ref, mat_ref)
    for c, part in enumerate(product(v_ref, mat_ref, vec_ref)):
        out_ref[:, c, 0] = first_ref[c].reshape(GROUP, SHOTS, ROWS)
        out_ref[:, c, 1] = part.reshape(GROUP, SHOTS, ROWS).astype(BF16)


def unpack(in_ref, out_ref):
    for c in range(2):
        for p in range(2):
            for h in range(ZH):
                for d in range(0, GROUP, 2):
                    pair = [in_ref[d + k, c, p, :, h * 64 : h * 64 + 64] for k in range(2)]
                    col = h * 512 + d * 64
                    out_ref[c, p, :, col : col + 128] = jnp.concatenate(pair, axis=-1)


def exchange(block, axes):
    return lax.all_to_all(block, axes, 0, 0, tiled=True)


def on_device(shot_fields, diag_inverse, coupling):
    group = ("zl", "x")
    block = array(2, GROUP_SHOTS, ROWS)
    repeated = array(GROUP, 2, GROUP_SHOTS, ROWS)

    mats = jnp.concatenate([diag_inverse.reshape(4, 64, 128), coupling])
    mats = lax.all_gather(mats, "zh", axis=0)
    mats = lax.all_gather(mats, ("y", "core"), axis=0)
    fields = call(pack, array(GROUP, 2, SHOTS, PANEL + ROWS), shot_fields)

    def stage(body, outs, sent, *args):
        scratch = [pltpu.VMEM((2 * ROWS, PANEL), BF16), pltpu.VMEM((2 * GROUP_SHOTS, PANEL), BF16)]
        flops = 2 * 2 * ROWS * PANEL * 2 * GROUP_SHOTS
        fields = exchange(sent, group)
        return call(body, outs, fields, mats, *args, scratch=scratch, flops=flops, moved=3 << 20)

    first_rep, first, second_slice = stage(first_stage, (repeated, block, block), fields)
    residual = stage(second_stage, repeated, first_rep, second_slice)
    both = stage(third_stage, array(GROUP, 2, 2, SHOTS, ROWS), residual, first)
    return call(unpack, array(2, 2, SHOTS, PANEL), exchange(both, group))


def solution(mesh):
    axes = ("zh", "zl", "x", "y", "core")
    fine = Mesh(mesh.devices.reshape(ZH, ZL, X, Y, CORES), axes)
    row, src = axes[:3], axes[3:]
    in_specs = (
        P(None, None, row + src, None),
        P(None, None, row, src),
        P(None, row, src),
    )
    out_specs = P(None, None, row + src, None)
    return jax.shard_map(
        on_device, mesh=fine, in_specs=in_specs, out_specs=out_specs, check_vma=False
    )
```
